32 devices in a mesh: seq: 16 (over z, y, core), grp: 2 (over x).
Axes of the slice: x: 2, y: 2, z: 4, core: 2. Of those that a mesh axis runs over, the one named last changes fastest.
Arguments:
- prompt_tokens: bfloat16 [16384, 2048], P('seq'), may hold values from -6 to 6
- response_tokens: bfloat16 [2, 16, 256, 2048], P('grp', 'seq'), may hold values from -6 to 6
- w_query: bfloat16 [2048, 1024], P('seq', 'grp'), may hold values from -0.125 to 0.125
- w_key: bfloat16 [2048, 1024], P('seq', 'grp'), may hold values from -0.125 to 0.125
- w_value: bfloat16 [2048, 2048], P('seq', 'grp'), may hold values from -0.125 to 0.125
- w_decay: bfloat16 [2048, 16], P('seq', 'grp'), may hold values from -0.125 to 0.125
- w_beta: bfloat16 [2048, 16], P('seq', 'grp'), may hold values from -0.125 to 0.125
- decay_rate: float32 [16], replicated, may hold values from 0 to 0.06
- beta_shift: float32 [16], replicated, may hold values from -9 to 1
- out_gain: float32 [128], replicated, may hold values from 0.25 to 1.75
- resp_lengths: int32 [2, 16], P('grp', 'seq'), may hold values from 1 to 256, 2048 in all within a row
Outputs:
- prompt_output: bfloat16 [16384, 2048], P('seq', 'grp')
- response_output: bfloat16 [2, 16, 256, 2048], P('grp', 'seq')
The draws below stay inside these ranges and needn't reach their ends.
Inputs may be any that keep to these rules, and one draw needn't show every extreme that they name: `resp_lengths`: in every group one response has exactly 256 tokens, and a group's lengths sum to 2048.
All inputs are finite; a program needn't handle non-finite values.
Results may differ from the reference program's by a relative error of at most 0.0062.
Values may be sent and summed in bfloat16 or wider, within the bound.
A program may use at most 128 MiB of HBM per device.

```python
import math
import jax
import jax.numpy as jnp
import numpy as np
from jax import lax

D = 2048
DK = 128
DV = 128
HK = 8
HV = 16
RLEN = 256
P_DEV = 1024
P_TOKENS = 16384
N_SEQ = 16
N_GRP = 2


def head_kinds(key):
    pick = jax.random.uniform(jax.random.fold_in(key, 71), (HV,), jnp.float32)
    first = jax.random.uniform(jax.random.fold_in(key, 72), (HV,), jnp.float32)
    second = jax.random.uniform(jax.random.fold_in(key, 73), (HV,), jnp.float32)
    slow = pick < 0.5
    return (slow, first, second)


def draw_decay_rate(key, part):
    slow, first, second = head_kinds(key)
    chain = P_DEV * N_SEQ
    slow_rate = 0.1 / chain * 5.0 ** first
    fast_rate = 0.025 * 2.4 ** second
    return jnp.where(slow, slow_rate, fast_rate).astype(jnp.float32)


def draw_beta_shift(key, part):
    slow, first, second = head_kinds(key)
    chain = P_DEV * N_SEQ
    slow_shift = jnp.log(DK / chain) - 1.0 + (second - 0.5)
    fast_shift = 2.0 * first - 1.0
    return jnp.where(slow, slow_shift, fast_shift).astype(jnp.float32)


def levels(key, shape, shards, least, top_value):
    def one(dim, blocks):
        steps = jax.random.uniform(jax.random.fold_in(jax.random.fold_in(key, 6), dim), (blocks,), jnp.float32, least / len(shards), top_value / len(shards))
        return jnp.repeat(jnp.exp(steps), shape[dim] // blocks).reshape((-1,) + (1,) * (len(shape) - dim - 1))

    factor_of = one(*shards[0])
    for cut in shards[1:]:
        factor_of = factor_of * one(*cut)
    return factor_of


def length_profile(number_of, total, reach, skew):
    loads = [(1 << 20) // math.isqrt(standing ** skew) + 1 for standing in range(2, number_of + 1)]
    spare, holding = total - reach - (number_of - 1), [1] * (number_of - 1)
    while spare > 0:
        free = [i for i in range(number_of - 1) if holding[i] < reach]
        pool, left = sum([loads[i] for i in free]), spare
        for i in free:
            more = min(reach - holding[i], max(1, left * loads[i] // pool), spare)
            holding[i] = holding[i] + more
            spare = spare - more
    return np.array([reach] + holding)


def uneven_parts(rng, count, total, most, lean):
    if count == 2:
        one = jax.random.randint(rng, (), max(1, total - most), min(most, total - 1) + 1)
        return jnp.stack([one, total - one])
    sizes = jnp.asarray(length_profile(count, total, most, lean), jnp.int32)
    twos = (count - 1) // 2
    giver, sink = sizes[1:1 + 2 * twos:2], sizes[2:2 + 2 * twos:2]
    slack = jnp.minimum(giver - 1, most - sink)
    passed = jax.random.randint(jax.random.fold_in(rng, 1), (twos,), 0, 1 << 20) % (slack + 1)
    sizes = sizes.at[1:1 + 2 * twos:2].set(giver - passed).at[2:2 + 2 * twos:2].set(sink + passed)
    return sizes[jax.random.permutation(jax.random.fold_in(rng, 2), count)]


def noise(stream_key, dims, spread, most, cuts=(), kind=jnp.bfloat16):
    factor_of = levels(stream_key, dims, cuts, -0.22, 0.18) if cuts else 1.0
    entries = jax.random.normal(stream_key, dims, jnp.float32) * spread * factor_of
    return jnp.minimum(jnp.maximum(entries, -most), most).astype(kind)


def setup_inputs(seed: int = 0) -> dict:
    streams_of = jax.random.split(jax.random.key(seed), 12)
    return {
        "prompt_tokens": noise(streams_of[0], (P_TOKENS, D), 1.0, 6.0, ((0, 16),)),
        "response_tokens": noise(streams_of[1], (N_GRP, N_SEQ, RLEN, D), 1.0, 6.0, ((0, 2), (1, 16))),
        "w_query": noise(streams_of[2], (D, HK * DK), D ** -0.5, 0.125, ((0, 16), (1, 2))),
        "w_key": noise(streams_of[3], (D, HK * DK), D ** -0.5, 0.125, ((0, 16), (1, 2))),
        "w_value": noise(streams_of[4], (D, HV * DV), D ** -0.5, 0.125, ((0, 16), (1, 2))),
        "w_decay": noise(streams_of[5], (D, HV), D ** -0.5, 0.125, ((0, 16), (1, 2))),
        "w_beta": noise(streams_of[6], (D, HV), D ** -0.5, 0.125, ((0, 16), (1, 2))),
        "decay_rate": draw_decay_rate(jax.random.fold_in(streams_of[11], 71), 0),
        "beta_shift": draw_beta_shift(jax.random.fold_in(streams_of[11], 71), 0),
        "out_gain": jnp.clip(1.0 + 0.15 * jax.random.normal(streams_of[9], (DV,), jnp.float32), 0.25, 1.75),
        "resp_lengths": jax.vmap(lambda own: uneven_parts(own, N_SEQ, N_SEQ * RLEN // 2, RLEN, 2))(jax.random.split(streams_of[10], N_GRP)).reshape((N_GRP, N_SEQ)).astype(jnp.int32),
    }


def make_heads(x, weights, rate, shift):
    raw = [jnp.dot(x, w, preferred_element_type=jnp.float32) for w in weights]
    count = x.shape[0]
    key_heads = raw[0].shape[1] // DK
    value_heads = raw[3].shape[1]
    repeat = value_heads // key_heads
    query_rows = raw[0].reshape(count, key_heads, DK)
    keys = raw[1].reshape(count, key_heads, DK)
    query_rows = query_rows * lax.rsqrt(lax.optimization_barrier(jnp.sum(query_rows * query_rows, axis=-1, keepdims=True)) + 1e-06) * DK ** (-0.5)
    keys = keys * lax.rsqrt(lax.optimization_barrier(jnp.sum(keys * keys, axis=-1, keepdims=True)) + 1e-06)
    query_rows = jnp.repeat(query_rows.astype(jnp.bfloat16), repeat, axis=1)
    keys = jnp.repeat(keys.astype(jnp.bfloat16), repeat, axis=1)
    values = raw[2].reshape(count, value_heads, raw[2].shape[1] // value_heads).astype(jnp.bfloat16)
    log_decay = -rate * jax.nn.softplus(raw[3])
    beta = jax.nn.sigmoid(raw[4] + shift)
    return (query_rows, keys, values, log_decay, beta)

def finish(layer_output, gain):
    normed = layer_output * lax.rsqrt(lax.optimization_barrier(jnp.mean(layer_output * layer_output, axis=-1, keepdims=True)) + 1e-06) * gain
    return normed.reshape(normed.shape[:-2] + (normed.shape[-2] * normed.shape[-1],)).astype(jnp.bfloat16)

def recur(query_rows, keys, values, log_decay, beta, state_matrix):
    highest_level = lax.Precision.HIGHEST

    def advance(state_matrix, inputs):
        query_current, key_current, v_now, g_now, b_now = inputs
        query_current = query_current.astype(jnp.float32)
        key_current = key_current.astype(jnp.float32)
        v_now = v_now.astype(jnp.float32)
        running_along = jnp.einsum('...yt,...ytl->...yl', key_current, state_matrix, precision=highest_level)
        scaled = b_now[..., None, None] * key_current[..., :, None]
        kept = state_matrix - scaled * running_along[..., None, :]
        state_matrix = jnp.exp(g_now)[..., None, None] * kept + scaled * v_now[..., None, :]
        layer_output = jnp.einsum('...wog,...wo->...wg', state_matrix, query_current, precision=highest_level)
        return (state_matrix, layer_output)
    return lax.scan(advance, state_matrix, (query_rows, keys, values, log_decay, beta))

def reference(prompt_tokens, response_tokens, w_query, w_key, w_value, w_decay, w_beta, decay_rate, beta_shift, out_gain, resp_lengths):
    weights = (w_query, w_key, w_value, w_decay, w_beta)
    query_rows, keys, values, log_decay, beta = make_heads(prompt_tokens, weights, decay_rate, beta_shift)
    start = jnp.zeros((HV, DK, DV), jnp.float32)
    end_state, prompt_out = recur(query_rows, keys, values, log_decay, beta, start)
    prompt_output = finish(prompt_out, out_gain)
    count = N_GRP * N_SEQ
    flat = response_tokens.reshape(count * RLEN, D)
    parts = make_heads(flat, weights, decay_rate, beta_shift)
    arranged = tuple((jnp.swapaxes(p.reshape((count, RLEN) + p.shape[1:]), 0, 1) for p in parts))
    init = jnp.broadcast_to(end_state, (count, HV, DK, DV))
    final_unused, outs = recur(arranged[0], arranged[1], arranged[2], arranged[3], arranged[4], init)
    outs = jnp.swapaxes(outs, 0, 1)
    finished = finish(outs, out_gain)
    positions = jnp.arange(RLEN, dtype=jnp.int32)
    live = positions[None, :] < resp_lengths.reshape(count)[:, None]
    masked = jnp.where(live[..., None], finished, jnp.zeros_like(finished))
    return (prompt_output, masked.reshape(N_GRP, N_SEQ, RLEN, HV * DV))
```

```python
import functools

import jax
import jax.numpy as jnp
from jax import lax
from jax.experimental import pallas as pl
from jax.experimental.pallas import tpu as pltpu
from jax.sharding import PartitionSpec as P

DK = 128
CHUNK = 128
ROWS = 256
LANES = 128
BF = jnp.bfloat16
F32 = jnp.float32


def dot(a, b):
    return jnp.dot(a, b, preferred_element_type=F32)


def dot_nt(a, b):
    return lax.dot_general(a, b, (((1,), (1,)), ((), ())), preferred_element_type=F32)


def block_kernel(
    key_heads, value_heads, span, x_ref, w_ref, rate_ref, shift_ref,
    out_ref, lift_ref, map_ref, raw, carry,
):
    repeat = value_heads // key_heads
    step = pl.program_id(0)
    heads = range(value_heads)
    row = lax.broadcasted_iota(jnp.int32, (CHUNK, CHUNK), 0)
    col = lax.broadcasted_iota(jnp.int32, (CHUNK, CHUNK), 1)
    ident = jnp.where(row == col, 1.0, 0.0).astype(F32)

    @pl.when(lax.rem(step, span) == 0)
    def _():
        for h in heads:
            carry[h, :, :DK] = ident
            carry[h, :, DK:] = jnp.zeros((DK, DK), F32)

    x = x_ref[...]
    total = w_ref.shape[1]
    for at in range(0, total, 512):
        size = min(512, total - at)
        raw[:, at:at + size] = dot(x, w_ref[:, at:at + size])

    @pl.loop(0, ROWS // CHUNK)
    def _(c):
        rows = pl.ds(pl.multiple_of(c * CHUNK, CHUNK), CHUNK)
        within = row >= col
        differ = row ^ col
        gates = raw[rows, total - LANES:]
        log_decay = -rate_ref[...] * jax.nn.softplus(gates)
        beta = jax.nn.sigmoid(gates + shift_ref[...])
        lower_ones = jnp.where(within, 1.0, 0.0).astype(F32)
        cumul = jnp.dot(
            lower_ones, log_decay, preferred_element_type=F32, precision=lax.Precision.HIGHEST
        )
        cumul_t = cumul.T
        beta_t = beta.T
        factor = jnp.exp(cumul)
        factor_t = jnp.exp(cumul_t)
        tail_t = jnp.exp(cumul_t[:, CHUNK - 1:] - cumul_t)
        masks = []
        size = 2
        while size < CHUNK:
            masks.append(
                jnp.where((differ >= size) & (differ < 2 * size) & within, 1.0, 0.0).astype(BF)
            )
            size *= 2

        queries, keys, keys_t, dots = [], [], [], []
        for j in range(key_heads):
            q = raw[rows, j * DK:(j + 1) * DK]
            k = raw[rows, (key_heads + j) * DK:(key_heads + j + 1) * DK]
            q = q * lax.rsqrt(jnp.sum(q * q, axis=-1, keepdims=True) + 1e-06) * DK ** (-0.5)
            k = k * lax.rsqrt(jnp.sum(k * k, axis=-1, keepdims=True) + 1e-06)
            q, k = q.astype(BF), k.astype(BF)
            queries.append(q.astype(F32))
            keys.append(k)
            keys_t.append(k.astype(F32).T)
            dots.append(dot_nt(jnp.concatenate([q, k], axis=0), k))

        lowers, inverses, scores = [], [], []
        for h in heads:
            both = dots[h // repeat]
            spread = cumul[:, h:h + 1] - cumul_t[h:h + 1, :]
            decay = jnp.where(within, jnp.exp(spread), 0.0)
            scores.append((decay * both[:CHUNK]).astype(BF))
            lower = jnp.where(
                differ > 0,
                beta[:, value_heads + h:value_heads + h + 1] * decay * both[CHUNK:],
                0.0,
            )
            inverses.append(ident - jnp.where(differ == 1, lower, 0.0))
            lowers.append(lower.astype(BF))
        for mask in masks:
            small = [x.astype(BF) for x in inverses]
            mids = [dot(lowers[h] * mask, small[h]).astype(BF) for h in heads]
            inverses = [inverses[h] - dot(small[h], mids[h]) for h in heads]

        solved = []
        for h in heads:
            b_row = beta_t[value_heads + h:value_heads + h + 1, :]
            scaled = inverses[h] * b_row
            at = (2 * key_heads + h) * DK
            values = raw[rows, at:at + DK].astype(BF)
            fresh = dot(scaled.astype(BF), values)
            weights = dot((scaled * factor_t[h:h + 1, :]).astype(BF), keys[h // repeat])
            solved.append(jnp.concatenate([weights, fresh], axis=1).astype(BF))
        parts = []
        for h in heads:
            tails = (keys_t[h // repeat] * tail_t[h:h + 1, :]).astype(BF)
            parts.append(dot(jnp.concatenate([scores[h], tails], axis=0), solved[h]))
        for h in heads:
            part = parts[h]
            lifted = factor[:, h:h + 1] * queries[h // repeat] - part[:CHUNK, :DK]
            state = carry[h]
            left = jnp.concatenate([lifted, -part[CHUNK:, :DK]], axis=0).astype(BF)
            moved = dot(left, state.astype(BF))
            last = factor[CHUNK - 1:, h:h + 1]
            span_cols = slice(h * DK, (h + 1) * DK)
            out_ref[rows, span_cols] = moved[:CHUNK, DK:] + part[:CHUNK, DK:]
            lift_ref[rows, span_cols] = moved[:CHUNK, :DK].astype(BF)
            fresh_state = last * state + moved[CHUNK:]
            carry[h, :, :DK] = fresh_state[:, :DK]
            carry[h, :, DK:] = fresh_state[:, DK:] + part[CHUNK:, DK:]

    @pl.when(step == pl.num_programs(0) - 1)
    def _():
        for h in heads:
            map_ref[h, :, :DK] = (carry[h, :, :DK] - ident).astype(BF)
            map_ref[h, :, DK:] = carry[h, :, DK:].astype(BF)


def run_blocks(x, weights, rate, shift, key_heads, value_heads, span):
    count, depth = x.shape
    total = weights.shape[1]
    width = value_heads * DK
    whole = lambda shape: pl.BlockSpec(shape, lambda i: (0,) * len(shape))
    return pl.pallas_call(
        functools.partial(block_kernel, key_heads, value_heads, span),
        grid=(count // ROWS,),
        in_specs=[
            pl.BlockSpec((ROWS, depth), lambda i: (i, 0)),
            pl.BlockSpec((depth, total), lambda i: (0, 0), pipeline_mode=pl.Buffered(1)),
            whole((1, LANES)),
            whole((1, LANES)),
        ],
        out_specs=[
            pl.BlockSpec((ROWS, width), lambda i: (i, 0)),
            pl.BlockSpec((ROWS, width), lambda i: (i, 0)),
            whole((value_heads, DK, 2 * DK)),
        ],
        out_shape=[
            jax.ShapeDtypeStruct((count, width), F32),
            jax.ShapeDtypeStruct((count, width), BF),
            jax.ShapeDtypeStruct((value_heads, DK, 2 * DK), BF),
        ],
        scratch_shapes=[
            pltpu.VMEM((ROWS, total), F32),
            pltpu.VMEM((value_heads, DK, 2 * DK), F32),
        ],
        compiler_params=pltpu.CompilerParams(
            dimension_semantics=("arbitrary",), vmem_limit_bytes=48 * 1024 * 1024
        ),
        cost_estimate=pl.CostEstimate(
            flops=2 * count * depth * total + 2 * count * width * 2600,
            bytes_accessed=2 * count * depth + 2 * depth * total + 6 * count * width,
            transcendentals=count * value_heads * DK,
        ),
    )(x, weights, rate, shift)


def scan_kernel(me_ref, maps_ref, start_ref, end_ref, state):
    step = pl.program_id(0)
    heads = range(state.shape[0])

    @pl.when(step == 0)
    def _():
        state[...] = jnp.zeros_like(state)

    @pl.when(step == me_ref[0])
    def _():
        start_ref[...] = state[...].astype(BF)

    for h in heads:
        held = state[h]
        high = held.astype(BF)
        low = (held - high.astype(F32)).astype(BF)
        moved = dot(maps_ref[0, h, :, :DK], jnp.concatenate([high, low], axis=1))
        state[h] = held + (moved[:, :DK] + moved[:, DK:]) + maps_ref[0, h, :, DK:].astype(F32)

    @pl.when(step == pl.num_programs(0) - 1)
    def _():
        end_ref[...] = state[...].astype(BF)


def run_scan(me, maps):
    count, heads = maps.shape[:2]
    one = pl.BlockSpec((heads, DK, DK), lambda i: (0, 0, 0))
    shape = jax.ShapeDtypeStruct((heads, DK, DK), BF)
    return pl.pallas_call(
        scan_kernel,
        grid=(count,),
        in_specs=[
            pl.BlockSpec(memory_space=pltpu.SMEM),
            pl.BlockSpec((1,) + maps.shape[1:], lambda i: (i, 0, 0, 0)),
        ],
        out_specs=[one, one],
        out_shape=[shape, shape],
        scratch_shapes=[pltpu.VMEM((heads, DK, DK), F32)],
        compiler_params=pltpu.CompilerParams(
            dimension_semantics=("arbitrary",), vmem_limit_bytes=32 * 1024 * 1024
        ),
    )(me, maps)


def finish_kernel(out_ref, lift_ref, state_ref, gain_ref, done_ref):
    for h in range(state_ref.shape[0]):
        cols = slice(h * DK, (h + 1) * DK)
        o = out_ref[:, cols] + dot(lift_ref[:, cols], state_ref[h])
        mean = jnp.mean(o * o, axis=-1, keepdims=True)
        done_ref[:, cols] = (o * lax.rsqrt(mean + 1e-06) * gain_ref[...]).astype(BF)


def run_finish(out, lifted, state, gain):
    count, width = out.shape
    rows = pl.BlockSpec((ROWS, width), lambda i: (i, 0))
    return pl.pallas_call(
        finish_kernel,
        grid=(count // ROWS,),
        in_specs=[
            rows,
            rows,
            pl.BlockSpec(state.shape, lambda i: (0, 0, 0)),
            pl.BlockSpec((1, DK), lambda i: (0, 0)),
        ],
        out_specs=rows,
        out_shape=jax.ShapeDtypeStruct((count, width), BF),
        compiler_params=pltpu.CompilerParams(
            dimension_semantics=("arbitrary",), vmem_limit_bytes=32 * 1024 * 1024
        ),
        cost_estimate=pl.CostEstimate(
            flops=2 * count * width * DK, bytes_accessed=8 * count * width, transcendentals=0
        ),
    )(out, lifted, state, gain)


def shards(
    n_grp,
    prompt_tokens,
    response_tokens,
    w_query,
    w_key,
    w_value,
    w_decay,
    w_beta,
    decay_rate,
    beta_shift,
    out_gain,
    resp_lengths,
):
    value_heads = w_decay.shape[1]
    key_heads = w_key.shape[1] // DK
    grp = lax.axis_index("grp")
    pad = LANES - 2 * value_heads
    first_head = grp * value_heads
    rate = lax.dynamic_slice_in_dim(decay_rate, first_head, value_heads)
    shift = lax.dynamic_slice_in_dim(beta_shift, first_head, value_heads)
    rate = jnp.pad(rate, (0, LANES - value_heads)).reshape(1, LANES)
    shift = jnp.pad(shift, (value_heads, pad)).reshape(1, LANES)
    gain = out_gain.reshape(1, DK)
    columns = jnp.concatenate(
        [w_query, w_key, w_value, w_decay, w_beta, jnp.zeros((w_decay.shape[0], pad), BF)], axis=1
    )
    weights = lax.all_gather(columns, "seq", axis=0, tiled=True)
    length, depth = response_tokens.shape[2:]
    tokens = lax.all_gather(response_tokens.reshape(length, depth), "grp", axis=0, tiled=True)

    blocks = prompt_tokens.shape[0] // ROWS
    out, lifted, own_map = run_blocks(
        prompt_tokens, weights, rate, shift, key_heads, value_heads, blocks
    )
    maps = lax.all_gather(own_map[None], "seq", axis=0, tiled=True)
    r_out, r_lifted, _ = run_blocks(
        tokens, weights, rate, shift, key_heads, value_heads, length // ROWS
    )
    start, end = run_scan(lax.axis_index("seq").reshape(1), maps)
    r_done = run_finish(r_out, r_lifted, end, gain).reshape(n_grp, length, -1)
    prompt_output = run_finish(out, lifted, start, gain)
    exchanged = lax.all_to_all(r_done, "grp", split_axis=0, concat_axis=0, tiled=True)
    finished = jnp.swapaxes(exchanged, 0, 1).reshape(length, -1)
    positions = lax.broadcasted_iota(jnp.int32, (length, 1), 0)
    masked = jnp.where(positions < resp_lengths.reshape(()), finished, jnp.zeros_like(finished))
    return (prompt_output, masked.reshape(1, 1, length, masked.shape[1]))


def solution(mesh):
    placed = (
        P("seq", None),
        P("grp", "seq", None, None),
        P("seq", "grp"),
        P("seq", "grp"),
        P("seq", "grp"),
        P("seq", "grp"),
        P("seq", "grp"),
        P(),
        P(),
        P(),
        P("grp", "seq"),
    )
    return jax.shard_map(
        functools.partial(shards, mesh.shape["grp"]),
        mesh=mesh,
        in_specs=placed,
        out_specs=(P("seq", "grp"), P("grp", "seq", None, None)),
        check_vma=False,
    )
```

```python
import functools

import jax
import jax.numpy as jnp
from jax import lax
from jax.experimental import pallas as pl
from jax.experimental.pallas import tpu as pltpu
from jax.sharding import PartitionSpec as P

DK = 128
CHUNK = 128
ROWS = 256
LANES = 128
BF = jnp.bfloat16
F32 = jnp.float32


def dot(a, b):
    return jnp.dot(a, b, preferred_element_type=F32)


def dot_nt(a, b):
    return lax.dot_general(a, b, (((1,), (1,)), ((), ())), preferred_element_type=F32)


def block_kernel(
    key_heads, value_heads, span, x_ref, w_ref, rate_ref, shift_ref,
    out_ref, lift_ref, map_ref, raw, carry,
):
    repeat = value_heads // key_heads
    step = pl.program_id(0)
    heads = range(value_heads)
    row = lax.broadcasted_iota(jnp.int32, (CHUNK, CHUNK), 0)
    col = lax.broadcasted_iota(jnp.int32, (CHUNK, CHUNK), 1)
    ident = jnp.where(row == col, 1.0, 0.0).astype(F32)

    @pl.when(lax.rem(step, span) == 0)
    def _():
        for h in heads:
            carry[h, :, :DK] = ident
            carry[h, :, DK:] = jnp.zeros((DK, DK), F32)

    x = x_ref[...]
    total = w_ref.shape[1]
    for at in range(0, total, 512):
        size = min(512, total - at)
        raw[:, at:at + size] = dot(x, w_ref[:, at:at + size])

    @pl.loop(0, ROWS // CHUNK)
    def _(c):
        rows = pl.ds(pl.multiple_of(c * CHUNK, CHUNK), CHUNK)
        within = row >= col
        differ = row ^ col
        gates = raw[rows, total - LANES:]
        log_decay = -rate_ref[...] * jax.nn.softplus(gates)
        beta = jax.nn.sigmoid(gates + shift_ref[...])
        lower_ones = jnp.where(within, 1.0, 0.0).astype(F32)
        cumul = jnp.dot(
            lower_ones, log_decay, preferred_element_type=F32, precision=lax.Precision.HIGHEST
        )
        cumul_t = cumul.T
        beta_t = beta.T
        factor = jnp.exp(cumul)
        factor_t = jnp.exp(cumul_t)
        tail_t = jnp.exp(cumul_t[:, CHUNK - 1:] - cumul_t)
        masks = []
        size = 2
        while size < CHUNK:
            masks.append(
                jnp.where((differ >= size) & (differ < 2 * size) & within, 1.0, 0.0).astype(BF)
            )
            size *= 2

        queries, keys, keys_t, dots = [], [], [], []
        for j in range(key_heads):
            q = raw[rows, j * DK:(j + 1) * DK]
            k = raw[rows, (key_heads + j) * DK:(key_heads + j + 1) * DK]
            q = q * lax.rsqrt(jnp.sum(q * q, axis=-1, keepdims=True) + 1e-06) * DK ** (-0.5)
            k = k * lax.rsqrt(jnp.sum(k * k, axis=-1, keepdims=True) + 1e-06)
            q, k = q.astype(BF), k.astype(BF)
            queries.append(q.astype(F32))
            keys.append(k)
            keys_t.append(k.astype(F32).T)
            dots.append(dot_nt(jnp.concatenate([q, k], axis=0), k))

        lowers, inverses, scores = [], [], []
        for h in heads:
            both = dots[h // repeat]
            spread = cumul[:, h:h + 1] - cumul_t[h:h + 1, :]
            decay = jnp.where(within, jnp.exp(spread), 0.0)
            scores.append((decay * both[:CHUNK]).astype(BF))
            lower = jnp.where(
                differ > 0,
                beta[:, value_heads + h:value_heads + h + 1] * decay * both[CHUNK:],
                0.0,
            )
            inverses.append(ident - jnp.where(differ == 1, lower, 0.0))
            lowers.append(lower.astype(BF))
        for mask in masks:
            small = [x.astype(BF) for x in inverses]
            mids = [dot(lowers[h] * mask, small[h]).astype(BF) for h in heads]
            inverses = [inverses[h] - dot(small[h], mids[h]) for h in heads]

        solved = []
        for h in heads:
            b_row = beta_t[value_heads + h:value_heads + h + 1, :]
            scaled = inverses[h] * b_row
            at = (2 * key_heads + h) * DK
            values = raw[rows, at:at + DK].astype(BF)
            fresh = dot(scaled.astype(BF), values)
            weights = dot((scaled * factor_t[h:h + 1, :]).astype(BF), keys[h // repeat])
            solved.append(jnp.concatenate([weights, fresh], axis=1).astype(BF))
        parts = []
        for h in heads:
            tails = (keys_t[h // repeat] * tail_t[h:h + 1, :]).astype(BF)
            parts.append(dot(jnp.concatenate([scores[h], tails], axis=0), solved[h]))
        for h in heads:
            part = parts[h]
            lifted = factor[:, h:h + 1] * queries[h // repeat] - part[:CHUNK, :DK]
            state = carry[h]
            left = jnp.concatenate([lifted, -part[CHUNK:, :DK]], axis=0).astype(BF)
            moved = dot(left, state.astype(BF))
            last = factor[CHUNK - 1:, h:h + 1]
            span_cols = slice(h * DK, (h + 1) * DK)
            out_ref[rows, span_cols] = moved[:CHUNK, DK:] + part[:CHUNK, DK:]
            lift_ref[rows, span_cols] = moved[:CHUNK, :DK].astype(BF)
            fresh_state = last * state + moved[CHUNK:]
            carry[h, :, :DK] = fresh_state[:, :DK]
            carry[h, :, DK:] = fresh_state[:, DK:] + part[CHUNK:, DK:]

    @pl.when(step == pl.num_programs(0) - 1)
    def _():
        parts = map_ref.shape[0] // value_heads
        width = DK // parts
        for h in heads:
            moves = (carry[h, :, :DK] - ident).astype(BF)
            ends = carry[h, :, DK:].T.astype(BF)
            for p in range(parts):
                map_ref[h * parts + p, :DK] = moves
                map_ref[h * parts + p, DK:] = ends[p * width:(p + 1) * width]


def run_blocks(x, weights, rate, shift, key_heads, value_heads, span, takers):
    count, depth = x.shape
    total = weights.shape[1]
    width = value_heads * DK
    map_rows = DK + DK * value_heads // takers
    whole = lambda shape: pl.BlockSpec(shape, lambda i: (0,) * len(shape))
    return pl.pallas_call(
        functools.partial(block_kernel, key_heads, value_heads, span),
        grid=(count // ROWS,),
        in_specs=[
            pl.BlockSpec((ROWS, depth), lambda i: (i, 0)),
            pl.BlockSpec((depth, total), lambda i: (0, 0), pipeline_mode=pl.Buffered(1)),
            whole((1, LANES)),
            whole((1, LANES)),
        ],
        out_specs=[
            pl.BlockSpec((ROWS, width), lambda i: (i, 0)),
            pl.BlockSpec((ROWS, width), lambda i: (i, 0)),
            whole((takers, map_rows, DK)),
        ],
        out_shape=[
            jax.ShapeDtypeStruct((count, width), F32),
            jax.ShapeDtypeStruct((count, width), BF),
            jax.ShapeDtypeStruct((takers, map_rows, DK), BF),
        ],
        scratch_shapes=[
            pltpu.VMEM((ROWS, total), F32),
            pltpu.VMEM((value_heads, DK, 2 * DK), F32),
        ],
        compiler_params=pltpu.CompilerParams(
            dimension_semantics=("arbitrary",), vmem_limit_bytes=48 * 1024 * 1024
        ),
        cost_estimate=pl.CostEstimate(
            flops=2 * count * depth * total + 2 * count * width * 2600,
            bytes_accessed=2 * count * depth + 2 * depth * total + 6 * count * width,
            transcendentals=count * value_heads * DK,
        ),
    )(x, weights, rate, shift)


def scan_kernel(maps_ref, states_ref):
    count, rows = maps_ref.shape[:2]
    held = jnp.zeros((rows - DK, DK), F32)
    for i in range(count):
        states_ref[i, 0] = held.astype(BF)
        high = held.astype(BF).astype(F32)
        both = jnp.concatenate([high, held - high], axis=0).astype(BF)
        moved = dot_nt(both, maps_ref[i, :DK])
        held = held + (moved[:rows - DK] + moved[rows - DK:]) + maps_ref[i, DK:].astype(F32)
    for i in range(count):
        states_ref[i, 1] = held.astype(BF)


def run_scan(maps):
    count, rows = maps.shape[:2]
    return pl.pallas_call(
        scan_kernel,
        out_shape=jax.ShapeDtypeStruct((count, 2, rows - DK, DK), BF),
        in_specs=[pl.BlockSpec(memory_space=pltpu.VMEM)],
        out_specs=pl.BlockSpec(memory_space=pltpu.VMEM),
        compiler_params=pltpu.CompilerParams(vmem_limit_bytes=16 * 1024 * 1024),
    )(maps)


def gather_kernel(count, own_ref, all_ref, own_sem, send_sems, recv_sems):
    size = own_ref.shape[0]
    me = lax.axis_index("seq")
    grp = lax.axis_index("grp")
    depth = count // 4
    z, place = lax.div(me, 4), lax.rem(me, 4)
    y, core = lax.div(place, 2), lax.rem(place, 2)
    across = z * 4 + (1 - y) * 2 + core
    twin = z * 4 + y * 2 + (1 - core)
    above, below = me + 4, me - 4

    def rows(block):
        return pl.ds(pl.multiple_of(block * size, size), size)

    def copy(block, way, target, source=None):
        return pltpu.make_async_remote_copy(
            src_ref=all_ref.at[rows(block)] if source is None else source,
            dst_ref=all_ref.at[rows(block)],
            send_sem=send_sems.at[block, way],
            recv_sem=recv_sems.at[block],
            device_id=(target, grp),
            device_id_type=pl.DeviceIdType.MESH,
        )

    def arrived(block):
        copy(block, 3, twin).wait_recv()

    barrier = pltpu.get_barrier_semaphore()

    def greet(target):
        pl.semaphore_signal(
            barrier, inc=1, device_id=(target, grp), device_id_type=pl.DeviceIdType.MESH
        )

    greet(across)
    greet(twin)

    @pl.when(z < depth - 1)
    def _():
        greet(above)

    @pl.when(z > 0)
    def _():
        greet(below)

    pl.semaphore_wait(
        barrier, 2 + jnp.where(z < depth - 1, 1, 0) + jnp.where(z > 0, 1, 0)
    )

    mine = pltpu.make_async_copy(own_ref, all_ref.at[rows(me)], own_sem)
    mine.start()

    @pl.when(z < depth - 1)
    def _():
        copy(me, 0, above, own_ref).start()

    @pl.when(z > 0)
    def _():
        copy(me, 1, below, own_ref).start()

    copy(me, 2, across, own_ref).start()
    copy(me, 3, twin, own_ref).start()

    for hop in range(1, depth):
        low, high = me - 4 * hop, me + 4 * hop

        @pl.when(z >= hop)
        def _():
            arrived(low)

            @pl.when(z < depth - 1)
            def _():
                copy(low, 0, above).start()

            copy(low, 2, across).start()
            copy(low, 3, twin).start()

        @pl.when(z + hop < depth)
        def _():
            arrived(high)

            @pl.when(z > 0)
            def _():
                copy(high, 1, below).start()

            copy(high, 2, across).start()
            copy(high, 3, twin).start()

        if hop == 1:
            arrived(across)
            copy(across, 3, twin).start()
        else:
            pass_on(across, hop - 1, z, depth, arrived, copy, twin)
    pass_on(across, depth - 1, z, depth, arrived, copy, twin)

    other = 1 - core
    for block in range(depth * 2):
        arrived(block * 2 + other)
    mine.wait()
    for up in range(depth):
        block = up * 4 + y * 2 + core

        @pl.when((up <= z) & (z < depth - 1))
        def _():
            copy(block, 0, above).wait_send()

        @pl.when((up >= z) & (z > 0))
        def _():
            copy(block, 1, below).wait_send()

        copy(block, 2, across).wait_send()
        copy(block, 3, twin).wait_send()
        copy(up * 4 + (1 - y) * 2 + core, 3, twin).wait_send()


def pass_on(across, hop, z, depth, arrived, copy, twin):
    @pl.when(z >= hop)
    def _():
        arrived(across - 4 * hop)
        copy(across - 4 * hop, 3, twin).start()

    @pl.when(z + hop < depth)
    def _():
        arrived(across + 4 * hop)
        copy(across + 4 * hop, 3, twin).start()


def run_gather(own, count):
    return pl.pallas_call(
        functools.partial(gather_kernel, count),
        out_shape=jax.ShapeDtypeStruct((count * own.shape[0], own.shape[1]), own.dtype),
        in_specs=[pl.BlockSpec(memory_space=pl.ANY)],
        out_specs=pl.BlockSpec(memory_space=pl.ANY),
        scratch_shapes=[
            pltpu.SemaphoreType.DMA,
            pltpu.SemaphoreType.DMA((count, 4)),
            pltpu.SemaphoreType.DMA((count,)),
        ],
        compiler_params=pltpu.CompilerParams(collective_id=0, has_side_effects=True),
        cost_estimate=pl.CostEstimate(
            flops=0, bytes_accessed=8 * count * own.size, transcendentals=0
        ),
    )(own)


def finish_kernel(out_ref, lift_ref, state_ref, gain_ref, done_ref):
    for h in range(state_ref.shape[0]):
        cols = slice(h * DK, (h + 1) * DK)
        o = out_ref[:, cols] + dot_nt(lift_ref[:, cols], state_ref[h])
        mean = jnp.mean(o * o, axis=-1, keepdims=True)
        done_ref[:, cols] = (o * lax.rsqrt(mean + 1e-06) * gain_ref[...]).astype(BF)


def run_finish(out, lifted, state, gain):
    count, width = out.shape
    rows = pl.BlockSpec((ROWS, width), lambda i: (i, 0))
    return pl.pallas_call(
        finish_kernel,
        grid=(count // ROWS,),
        in_specs=[
            rows,
            rows,
            pl.BlockSpec(state.shape, lambda i: (0, 0, 0)),
            pl.BlockSpec((1, DK), lambda i: (0, 0)),
        ],
        out_specs=rows,
        out_shape=jax.ShapeDtypeStruct((count, width), BF),
        compiler_params=pltpu.CompilerParams(
            dimension_semantics=("arbitrary",), vmem_limit_bytes=32 * 1024 * 1024
        ),
        cost_estimate=pl.CostEstimate(
            flops=2 * count * width * DK, bytes_accessed=8 * count * width, transcendentals=0
        ),
    )(out, lifted, state, gain)


def shards(
    n_seq,
    n_grp,
    prompt_tokens,
    response_tokens,
    w_query,
    w_key,
    w_value,
    w_decay,
    w_beta,
    decay_rate,
    beta_shift,
    out_gain,
    resp_lengths,
):
    value_heads = w_decay.shape[1]
    key_heads = w_key.shape[1] // DK
    grp = lax.axis_index("grp")
    pad = LANES - 2 * value_heads
    first_head = grp * value_heads
    rate = lax.dynamic_slice_in_dim(decay_rate, first_head, value_heads)
    shift = lax.dynamic_slice_in_dim(beta_shift, first_head, value_heads)
    rate = jnp.pad(rate, (0, LANES - value_heads)).reshape(1, LANES)
    shift = jnp.pad(shift, (value_heads, pad)).reshape(1, LANES)
    gain = out_gain.reshape(1, DK)
    columns = jnp.concatenate(
        [w_query, w_key, w_value, w_decay, w_beta, jnp.zeros((w_decay.shape[0], pad), BF)], axis=1
    )
    weights = run_gather(columns, n_seq)
    length, depth = response_tokens.shape[2:]
    tokens = lax.all_gather(response_tokens.reshape(length, depth), "grp", axis=0, tiled=True)

    blocks = prompt_tokens.shape[0] // ROWS
    out, lifted, own_map = run_blocks(
        prompt_tokens, weights, rate, shift, key_heads, value_heads, blocks, n_seq
    )
    maps = lax.all_to_all(own_map, "seq", split_axis=0, concat_axis=0, tiled=True)
    r_out, r_lifted, _ = run_blocks(
        tokens, weights, rate, shift, key_heads, value_heads, length // ROWS, value_heads
    )
    states = lax.all_to_all(run_scan(maps), "seq", split_axis=0, concat_axis=0, tiled=True)
    start = states[:, 0].reshape(value_heads, DK, DK)
    end = states[:, 1].reshape(value_heads, DK, DK)
    r_done = run_finish(r_out, r_lifted, end, gain).reshape(n_grp, length, -1)
    prompt_output = run_finish(out, lifted, start, gain)
    exchanged = lax.all_to_all(r_done, "grp", split_axis=0, concat_axis=0, tiled=True)
    finished = jnp.swapaxes(exchanged, 0, 1).reshape(length, -1)
    positions = lax.broadcasted_iota(jnp.int32, (length, 1), 0)
    masked = jnp.where(positions < resp_lengths.reshape(()), finished, jnp.zeros_like(finished))
    return (prompt_output, masked.reshape(1, 1, length, masked.shape[1]))


def solution(mesh):
    placed = (
        P("seq", None),
        P("grp", "seq", None, None),
        P("seq", "grp"),
        P("seq", "grp"),
        P("seq", "grp"),
        P("seq", "grp"),
        P("seq", "grp"),
        P(),
        P(),
        P(),
        P("grp", "seq"),
    )
    return jax.shard_map(
        functools.partial(shards, mesh.shape["seq"], mesh.shape["grp"]),
        mesh=mesh,
        in_specs=placed,
        out_specs=(P("seq", "grp"), P("grp", "seq", None, None)),
        check_vma=False,
    )
```

```python
import functools

import jax
import jax.numpy as jnp
from jax import lax
from jax.experimental import pallas as pl
from jax.experimental.pallas import tpu as pltpu
from jax.sharding import PartitionSpec as P

DK = 128
CHUNK = 128
ROWS = 256
LANES = 128
BF = jnp.bfloat16
F32 = jnp.float32


def dot(a, b):
    return jnp.dot(a, b, preferred_element_type=F32)


def dot_nt(a, b):
    return lax.dot_general(a, b, (((1,), (1,)), ((), ())), preferred_element_type=F32)


def block_kernel(
    key_heads, value_heads, first, local, span, x_ref, w_ref, gate_ref, rate_ref, shift_ref,
    out_ref, lift_ref, map_ref, raw, carry,
):
    repeat = value_heads // key_heads
    step = pl.program_id(0)
    heads = range(value_heads)
    row = lax.broadcasted_iota(jnp.int32, (CHUNK, CHUNK), 0)
    col = lax.broadcasted_iota(jnp.int32, (CHUNK, CHUNK), 1)
    ident = jnp.where(row == col, 1.0, 0.0).astype(F32)

    @pl.when(lax.rem(step, span) == 0)
    def _():
        for h in heads:
            carry[h, :, :DK] = ident
            carry[h, :, DK:] = jnp.zeros((DK, DK), F32)

    x = x_ref[...]
    total = w_ref.shape[1]
    for at in range(0, total, 512):
        size = min(512, total - at)
        raw[:, at:at + size] = dot(x, w_ref[:, at:at + size])
    raw[:, total:] = dot(x, gate_ref[...])

    @pl.loop(0, ROWS // CHUNK)
    def _(c):
        rows = pl.ds(pl.multiple_of(c * CHUNK, CHUNK), CHUNK)
        within = row >= col
        differ = row ^ col
        gates = raw[rows, total:]
        log_decay = -rate_ref[...] * jax.nn.softplus(gates)
        beta = jax.nn.sigmoid(gates + shift_ref[...])
        lower_ones = jnp.where(within, 1.0, 0.0).astype(F32)
        cumul = jnp.dot(
            lower_ones, log_decay, preferred_element_type=F32, precision=lax.Precision.HIGHEST
        )
        cumul_t = cumul.T
        beta_t = beta.T
        factor = jnp.exp(cumul)
        factor_t = jnp.exp(cumul_t)
        tail_t = jnp.exp(cumul_t[:, CHUNK - 1:] - cumul_t)
        masks = []
        size = 2
        while size < CHUNK:
            masks.append(
                jnp.where((differ >= size) & (differ < 2 * size) & within, 1.0, 0.0).astype(BF)
            )
            size *= 2

        queries, keys, keys_t, dots = [], [], [], []
        for j in range(key_heads):
            q = raw[rows, j * DK:(j + 1) * DK]
            k = raw[rows, (key_heads + j) * DK:(key_heads + j + 1) * DK]
            q = q * lax.rsqrt(jnp.sum(q * q, axis=-1, keepdims=True) + 1e-06) * DK ** (-0.5)
            k = k * lax.rsqrt(jnp.sum(k * k, axis=-1, keepdims=True) + 1e-06)
            q, k = q.astype(BF), k.astype(BF)
            queries.append(q.astype(F32))
            keys.append(k)
            keys_t.append(k.astype(F32).T)
            dots.append(dot_nt(jnp.concatenate([q, k], axis=0), k))

        lowers, inverses, scores = [], [], []
        for h in heads:
            both = dots[h // repeat]
            g = first + h
            spread = cumul[:, g:g + 1] - cumul_t[g:g + 1, :]
            decay = jnp.where(within, jnp.exp(spread), 0.0)
            scores.append((decay * both[:CHUNK]).astype(BF))
            lower = jnp.where(
                differ > 0,
                beta[:, local + g:local + g + 1] * decay * both[CHUNK:],
                0.0,
            )
            inverses.append(ident - jnp.where(differ == 1, lower, 0.0))
            lowers.append(lower.astype(BF))
        for mask in masks:
            small = [x.astype(BF) for x in inverses]
            mids = [dot(lowers[h] * mask, small[h]).astype(BF) for h in heads]
            inverses = [inverses[h] - dot(small[h], mids[h]) for h in heads]

        solved = []
        for h in heads:
            g = first + h
            b_row = beta_t[local + g:local + g + 1, :]
            scaled = inverses[h] * b_row
            at = (2 * key_heads + h) * DK
            values = raw[rows, at:at + DK].astype(BF)
            fresh = dot(scaled.astype(BF), values)
            weights = dot((scaled * factor_t[g:g + 1, :]).astype(BF), keys[h // repeat])
            solved.append(jnp.concatenate([weights, fresh], axis=1).astype(BF))
        parts = []
        for h in heads:
            g = first + h
            tails = (keys_t[h // repeat] * tail_t[g:g + 1, :]).astype(BF)
            parts.append(dot(jnp.concatenate([scores[h], tails], axis=0), solved[h]))
        for h in heads:
            g = first + h
            part = parts[h]
            lifted = factor[:, g:g + 1] * queries[h // repeat] - part[:CHUNK, :DK]
            state = carry[h]
            left = jnp.concatenate([lifted, -part[CHUNK:, :DK]], axis=0).astype(BF)
            moved = dot(left, state.astype(BF))
            last = factor[CHUNK - 1:, g:g + 1]
            span_cols = slice(h * DK, (h + 1) * DK)
            out_ref[rows, span_cols] = moved[:CHUNK, DK:] + part[:CHUNK, DK:]
            lift_ref[rows, span_cols] = moved[:CHUNK, :DK].astype(BF)
            fresh_state = last * state + moved[CHUNK:]
            carry[h, :, :DK] = fresh_state[:, :DK]
            carry[h, :, DK:] = fresh_state[:, DK:] + part[CHUNK:, DK:]

    @pl.when(step == pl.num_programs(0) - 1)
    def _():
        parts = map_ref.shape[0] // value_heads
        width = DK // parts
        for h in heads:
            moves = (carry[h, :, :DK] - ident).astype(BF)
            ends = carry[h, :, DK:].T.astype(BF)
            for p in range(parts):
                map_ref[h * parts + p, :DK] = moves
                map_ref[h * parts + p, DK:] = ends[p * width:(p + 1) * width]


def run_blocks(x, weights, gates, rate, shift, sizes, span, takers):
    key_heads, value_heads, first, local = sizes
    count, depth = x.shape
    total = (2 * key_heads + value_heads) * DK
    gate_block = gates.shape[1] // LANES - 1
    width = value_heads * DK
    map_rows = DK + DK * value_heads // takers
    whole = lambda shape: pl.BlockSpec(shape, lambda i: (0,) * len(shape))
    return pl.pallas_call(
        functools.partial(block_kernel, key_heads, value_heads, first, local, span),
        grid=(count // ROWS,),
        in_specs=[
            pl.BlockSpec((ROWS, depth), lambda i: (i, 0)),
            pl.BlockSpec((depth, total), lambda i: (0, 0), pipeline_mode=pl.Buffered(1)),
            pl.BlockSpec(
                (depth, LANES), lambda i: (0, gate_block), pipeline_mode=pl.Buffered(1)
            ),
            whole((1, LANES)),
            whole((1, LANES)),
        ],
        out_specs=[
            pl.BlockSpec((ROWS, width), lambda i: (i, 0)),
            pl.BlockSpec((ROWS, width), lambda i: (i, 0)),
            whole((takers, map_rows, DK)),
        ],
        out_shape=[
            jax.ShapeDtypeStruct((count, width), F32),
            jax.ShapeDtypeStruct((count, width), BF),
            jax.ShapeDtypeStruct((takers, map_rows, DK), BF),
        ],
        scratch_shapes=[
            pltpu.VMEM((ROWS, total + LANES), F32),
            pltpu.VMEM((value_heads, DK, 2 * DK), F32),
        ],
        compiler_params=pltpu.CompilerParams(
            dimension_semantics=("arbitrary",), vmem_limit_bytes=48 * 1024 * 1024
        ),
        cost_estimate=pl.CostEstimate(
            flops=2 * count * depth * total + 2 * count * width * 2600,
            bytes_accessed=2 * count * depth + 2 * depth * total + 6 * count * width,
            transcendentals=count * value_heads * DK,
        ),
    )(x, weights, gates, rate, shift)


def scan_kernel(*refs):
    maps, states_ref = refs[:-1], refs[-1]
    count, rows = maps[0].shape[:2]
    width = rows - DK
    held = [jnp.zeros((width, DK), F32) for _ in maps]
    for i in range(count):
        for p, ref in enumerate(maps):
            states_ref[i, 2 * p] = held[p].astype(BF)
            high = held[p].astype(BF).astype(F32)
            both = jnp.concatenate([high, held[p] - high], axis=0).astype(BF)
            moved = dot_nt(both, ref[i, :DK])
            held[p] = held[p] + (moved[:width] + moved[width:]) + ref[i, DK:].astype(F32)
    for i in range(count):
        for p in range(len(maps)):
            states_ref[i, 2 * p + 1] = held[p].astype(BF)


def run_scan(maps):
    count, rows = maps[0].shape[:2]
    return pl.pallas_call(
        scan_kernel,
        out_shape=jax.ShapeDtypeStruct((count, 2 * len(maps), rows - DK, DK), BF),
        in_specs=[pl.BlockSpec(memory_space=pltpu.VMEM)] * len(maps),
        out_specs=pl.BlockSpec(memory_space=pltpu.VMEM),
        compiler_params=pltpu.CompilerParams(vmem_limit_bytes=16 * 1024 * 1024),
    )(*maps)


def gather_kernel(count, own_ref, all_ref, own_sem, send_sems, recv_sems):
    size = own_ref.shape[0]
    me = lax.axis_index("seq")
    grp = lax.axis_index("grp")
    depth = count // 4
    z, place = lax.div(me, 4), lax.rem(me, 4)
    y, core = lax.div(place, 2), lax.rem(place, 2)
    across = z * 4 + (1 - y) * 2 + core
    twin = z * 4 + y * 2 + (1 - core)
    above, below = me + 4, me - 4

    def rows(block):
        return pl.ds(pl.multiple_of(block * size, size), size)

    def copy(block, way, target, source=None):
        return pltpu.make_async_remote_copy(
            src_ref=all_ref.at[rows(block)] if source is None else source,
            dst_ref=all_ref.at[rows(block)],
            send_sem=send_sems.at[block, way],
            recv_sem=recv_sems.at[block],
            device_id=(target, grp),
            device_id_type=pl.DeviceIdType.MESH,
        )

    def arrived(block):
        copy(block, 3, twin).wait_recv()

    barrier = pltpu.get_barrier_semaphore()

    def greet(target):
        pl.semaphore_signal(
            barrier, inc=1, device_id=(target, grp), device_id_type=pl.DeviceIdType.MESH
        )

    greet(across)
    greet(twin)

    @pl.when(z < depth - 1)
    def _():
        greet(above)

    @pl.when(z > 0)
    def _():
        greet(below)

    pl.semaphore_wait(
        barrier, 2 + jnp.where(z < depth - 1, 1, 0) + jnp.where(z > 0, 1, 0)
    )

    mine = pltpu.make_async_copy(own_ref, all_ref.at[rows(me)], own_sem)
    mine.start()

    @pl.when(z < depth - 1)
    def _():
        copy(me, 0, above, own_ref).start()

    @pl.when(z > 0)
    def _():
        copy(me, 1, below, own_ref).start()

    copy(me, 2, across, own_ref).start()
    copy(me, 3, twin, own_ref).start()

    for hop in range(1, depth):
        low, high = me - 4 * hop, me + 4 * hop

        @pl.when(z >= hop)
        def _():
            arrived(low)

            @pl.when(z < depth - 1)
            def _():
                copy(low, 0, above).start()

            copy(low, 2, across).start()
            copy(low, 3, twin).start()

        @pl.when(z + hop < depth)
        def _():
            arrived(high)

            @pl.when(z > 0)
            def _():
                copy(high, 1, below).start()

            copy(high, 2, across).start()
            copy(high, 3, twin).start()

        if hop == 1:
            arrived(across)
            copy(across, 3, twin).start()
        else:
            pass_on(across, hop - 1, z, depth, arrived, copy, twin)
    pass_on(across, depth - 1, z, depth, arrived, copy, twin)

    other = 1 - core
    for block in range(depth * 2):
        arrived(block * 2 + other)
    mine.wait()
    for up in range(depth):
        block = up * 4 + y * 2 + core

        @pl.when((up <= z) & (z < depth - 1))
        def _():
            copy(block, 0, above).wait_send()

        @pl.when((up >= z) & (z > 0))
        def _():
            copy(block, 1, below).wait_send()

        copy(block, 2, across).wait_send()
        copy(block, 3, twin).wait_send()
        copy(up * 4 + (1 - y) * 2 + core, 3, twin).wait_send()


def pass_on(across, hop, z, depth, arrived, copy, twin):
    @pl.when(z >= hop)
    def _():
        arrived(across - 4 * hop)
        copy(across - 4 * hop, 3, twin).start()

    @pl.when(z + hop < depth)
    def _():
        arrived(across + 4 * hop)
        copy(across + 4 * hop, 3, twin).start()


def run_gather(own, count):
    return pl.pallas_call(
        functools.partial(gather_kernel, count),
        out_shape=jax.ShapeDtypeStruct((count * own.shape[0], own.shape[1]), own.dtype),
        in_specs=[pl.BlockSpec(memory_space=pl.ANY)],
        out_specs=pl.BlockSpec(memory_space=pl.ANY),
        scratch_shapes=[
            pltpu.SemaphoreType.DMA,
            pltpu.SemaphoreType.DMA((count, 4)),
            pltpu.SemaphoreType.DMA((count,)),
        ],
        compiler_params=pltpu.CompilerParams(collective_id=0, has_side_effects=True),
        cost_estimate=pl.CostEstimate(
            flops=0, bytes_accessed=8 * count * own.size, transcendentals=0
        ),
    )(own)


def finish_kernel(*refs):
    gain_ref, done_ref = refs[-2:]
    parts = (len(refs) - 2) // 3
    outs, lifts, states = refs[:parts], refs[parts:2 * parts], refs[2 * parts:3 * parts]
    at = 0
    for out_ref, lift_ref, state_ref in zip(outs, lifts, states):
        for h in range(state_ref.shape[0]):
            cols = slice(h * DK, (h + 1) * DK)
            o = out_ref[:, cols] + dot_nt(lift_ref[:, cols], state_ref[h])
            mean = jnp.mean(o * o, axis=-1, keepdims=True)
            done_ref[:, at:at + DK] = (o * lax.rsqrt(mean + 1e-06) * gain_ref[...]).astype(BF)
            at += DK


def run_finish(outs, lifts, states, gain):
    count = outs[0].shape[0]
    width = sum(o.shape[1] for o in outs)
    rows = [pl.BlockSpec((ROWS, o.shape[1]), lambda i: (i, 0)) for o in outs]
    return pl.pallas_call(
        finish_kernel,
        grid=(count // ROWS,),
        in_specs=rows + rows
        + [pl.BlockSpec(s.shape, lambda i: (0, 0, 0)) for s in states]
        + [pl.BlockSpec((1, DK), lambda i: (0, 0))],
        out_specs=pl.BlockSpec((ROWS, width), lambda i: (i, 0)),
        out_shape=jax.ShapeDtypeStruct((count, width), BF),
        compiler_params=pltpu.CompilerParams(
            dimension_semantics=("arbitrary",), vmem_limit_bytes=32 * 1024 * 1024
        ),
        cost_estimate=pl.CostEstimate(
            flops=2 * count * width * DK, bytes_accessed=8 * count * width, transcendentals=0
        ),
    )(*outs, *lifts, *states, gain)


def shards(
    n_seq,
    n_grp,
    prompt_tokens,
    response_tokens,
    w_query,
    w_key,
    w_value,
    w_decay,
    w_beta,
    decay_rate,
    beta_shift,
    out_gain,
    resp_lengths,
):
    value_heads = w_decay.shape[1]
    key_heads = w_key.shape[1] // DK
    grp = lax.axis_index("grp")
    pad = LANES - 2 * value_heads
    first_head = grp * value_heads
    rate = lax.dynamic_slice_in_dim(decay_rate, first_head, value_heads)
    shift = lax.dynamic_slice_in_dim(beta_shift, first_head, value_heads)
    rate = jnp.pad(rate, (0, LANES - value_heads)).reshape(1, LANES)
    shift = jnp.pad(shift, (value_heads, pad)).reshape(1, LANES)
    gain = out_gain.reshape(1, DK)
    parts = 2 if key_heads % 2 == 0 else 1
    part_heads = value_heads // parts

    def part_of(array, part):
        size = array.shape[1] // parts
        return array[:, part * size:(part + 1) * size]

    columns = [[part_of(w, p) for w in (w_query, w_key, w_value)] for p in range(parts)]
    columns[0] += [w_decay, w_beta, jnp.zeros((w_decay.shape[0], pad), BF)]
    columns = [jnp.concatenate(group, axis=1) for group in columns]
    weights = [run_gather(columns[0], n_seq)]
    weights += [lax.all_gather(c, "seq", axis=0, tiled=True) for c in columns[1:]]
    length, depth = response_tokens.shape[2:]
    tokens = lax.all_gather(response_tokens.reshape(length, depth), "grp", axis=0, tiled=True)

    def blocks_of(x, part, span, takers):
        sizes = (key_heads // parts, part_heads, part * part_heads, value_heads)
        return run_blocks(x, weights[part], weights[0], rate, shift, sizes, span, takers)

    blocks = prompt_tokens.shape[0] // ROWS
    outs, lifts, maps, r_outs, r_lifts = [], [], [], [], []
    for p in range(parts):
        out, lifted, own_map = blocks_of(prompt_tokens, p, blocks, n_seq)
        outs.append(out)
        lifts.append(lifted)
        maps.append(lax.all_to_all(own_map, "seq", split_axis=0, concat_axis=0, tiled=True))
    for p in range(parts):
        if p == parts - 1:
            maps, r_outs, r_lifts = lax.optimization_barrier((maps, r_outs, r_lifts))
            chained = run_scan(maps)
            chained, tokens = lax.optimization_barrier((chained, tokens))
            states = lax.all_to_all(chained, "seq", split_axis=0, concat_axis=0, tiled=True)
        r_out, r_lifted, _ = blocks_of(tokens, p, length // ROWS, part_heads)
        r_outs.append(r_out)
        r_lifts.append(r_lifted)
    starts = [states[:, 2 * p].reshape(part_heads, DK, DK) for p in range(parts)]
    ends = [states[:, 2 * p + 1].reshape(part_heads, DK, DK) for p in range(parts)]
    r_done = run_finish(r_outs, r_lifts, ends, gain).reshape(n_grp, length, -1)
    prompt_output = run_finish(outs, lifts, starts, gain)
    exchanged = lax.all_to_all(r_done, "grp", split_axis=0, concat_axis=0, tiled=True)
    finished = jnp.swapaxes(exchanged, 0, 1).reshape(length, -1)
    positions = lax.broadcasted_iota(jnp.int32, (length, 1), 0)
    masked = jnp.where(positions < resp_lengths.reshape(()), finished, jnp.zeros_like(finished))
    return (prompt_output, masked.reshape(1, 1, length, masked.shape[1]))


def solution(mesh):
    placed = (
        P("seq", None),
        P("grp", "seq", None, None),
        P("seq", "grp"),
        P("seq", "grp"),
        P("seq", "grp"),
        P("seq", "grp"),
        P("seq", "grp"),
        P(),
        P(),
        P(),
        P("grp", "seq"),
    )
    return jax.shard_map(
        functools.partial(shards, mesh.shape["seq"], mesh.shape["grp"]),
        mesh=mesh,
        in_specs=placed,
        out_specs=(P("seq", "grp"), P("grp", "seq", None, None)),
        check_vma=False,
    )
```

```python
import functools

import jax
import jax.numpy as jnp
from jax import lax
from jax.experimental import pallas as pl
from jax.experimental.pallas import tpu as pltpu
from jax.sharding import PartitionSpec as P

DK = 128
CHUNK = 128
ROWS = 256
LANES = 128
BF = jnp.bfloat16
F32 = jnp.float32


def dot(a, b):
    return jnp.dot(a, b, preferred_element_type=F32)


def dot_nt(a, b):
    return lax.dot_general(a, b, (((1,), (1,)), ((), ())), preferred_element_type=F32)


def block_kernel(
    key_heads, value_heads, span, x_ref, w_ref, rate_ref, shift_ref,
    out_ref, lift_ref, map_ref, raw, carry,
):
    repeat = value_heads // key_heads
    step = pl.program_id(0)
    heads = range(value_heads)
    row = lax.broadcasted_iota(jnp.int32, (CHUNK, CHUNK), 0)
    col = lax.broadcasted_iota(jnp.int32, (CHUNK, CHUNK), 1)
    ident = jnp.where(row == col, 1.0, 0.0).astype(F32)

    @pl.when(lax.rem(step, span) == 0)
    def _():
        for h in heads:
            carry[h, :, :DK] = ident
            carry[h, :, DK:] = jnp.zeros((DK, DK), F32)

    x = x_ref[...]
    total = w_ref.shape[1]
    for at in range(0, total, 512):
        size = min(512, total - at)
        raw[:, at:at + size] = dot(x, w_ref[:, at:at + size])

    within = row >= col
    differ = row ^ col
    lower_ones = jnp.where(within, 1.0, 0.0).astype(F32)
    masks = []
    size = 2
    while size < CHUNK:
        masks.append(
            jnp.where((differ >= size) & (differ < 2 * size) & within, 1.0, 0.0).astype(BF)
        )
        size *= 2

    chunks = range(ROWS // CHUNK)
    both_of = [(c, h) for c in chunks for h in heads]
    gates_of, queries, keys, keys_t, dots = [], {}, {}, {}, {}
    for c in chunks:
        rows = slice(c * CHUNK, (c + 1) * CHUNK)
        gates = raw[rows, total - LANES:]
        log_decay = -rate_ref[...] * jax.nn.softplus(gates)
        beta = jax.nn.sigmoid(gates + shift_ref[...])
        cumul = jnp.dot(
            lower_ones, log_decay, preferred_element_type=F32, precision=lax.Precision.HIGHEST
        )
        cumul_t = cumul.T
        gates_of.append(
            (
                beta,
                beta.T,
                cumul,
                cumul_t,
                jnp.exp(cumul),
                jnp.exp(cumul_t),
                jnp.exp(cumul_t[:, CHUNK - 1:] - cumul_t),
            )
        )
        for j in range(key_heads):
            q = raw[rows, j * DK:(j + 1) * DK]
            k = raw[rows, (key_heads + j) * DK:(key_heads + j + 1) * DK]
            q = q * lax.rsqrt(jnp.sum(q * q, axis=-1, keepdims=True) + 1e-06) * DK ** (-0.5)
            k = k * lax.rsqrt(jnp.sum(k * k, axis=-1, keepdims=True) + 1e-06)
            q, k = q.astype(BF), k.astype(BF)
            queries[c, j] = q.astype(F32)
            keys[c, j] = k
            keys_t[c, j] = k.astype(F32).T
            dots[c, j] = dot_nt(jnp.concatenate([q, k], axis=0), k)

    lowers, inverses, scores = {}, {}, {}
    for c, h in both_of:
        beta, _, cumul, cumul_t = gates_of[c][:4]
        both = dots[c, h // repeat]
        spread = cumul[:, h:h + 1] - cumul_t[h:h + 1, :]
        decay = jnp.where(within, jnp.exp(spread), 0.0)
        scores[c, h] = (decay * both[:CHUNK]).astype(BF)
        lower = jnp.where(
            differ > 0,
            beta[:, value_heads + h:value_heads + h + 1] * decay * both[CHUNK:],
            0.0,
        )
        inverses[c, h] = ident - jnp.where(differ == 1, lower, 0.0)
        lowers[c, h] = lower.astype(BF)
    for mask in masks:
        small = {i: inverses[i].astype(BF) for i in both_of}
        mids = {i: dot(lowers[i] * mask, small[i]).astype(BF) for i in both_of}
        inverses = {i: inverses[i] - dot(small[i], mids[i]) for i in both_of}

    solved, parts = {}, {}
    for c, h in both_of:
        beta_t, factor_t = gates_of[c][1], gates_of[c][5]
        scaled = inverses[c, h] * beta_t[value_heads + h:value_heads + h + 1, :]
        at = (2 * key_heads + h) * DK
        values = raw[c * CHUNK:(c + 1) * CHUNK, at:at + DK].astype(BF)
        fresh = dot(scaled.astype(BF), values)
        weights = dot((scaled * factor_t[h:h + 1, :]).astype(BF), keys[c, h // repeat])
        solved[c, h] = jnp.concatenate([weights, fresh], axis=1).astype(BF)
    for c, h in both_of:
        tail_t = gates_of[c][6]
        tails = (keys_t[c, h // repeat] * tail_t[h:h + 1, :]).astype(BF)
        parts[c, h] = dot(jnp.concatenate([scores[c, h], tails], axis=0), solved[c, h])
    for c, h in both_of:
        factor = gates_of[c][4]
        rows, span_cols = slice(c * CHUNK, (c + 1) * CHUNK), slice(h * DK, (h + 1) * DK)
        part = parts[c, h]
        lifted = factor[:, h:h + 1] * queries[c, h // repeat] - part[:CHUNK, :DK]
        state = carry[h]
        left = jnp.concatenate([lifted, -part[CHUNK:, :DK]], axis=0).astype(BF)
        moved = dot(left, state.astype(BF))
        last = factor[CHUNK - 1:, h:h + 1]
        out_ref[rows, span_cols] = moved[:CHUNK, DK:] + part[:CHUNK, DK:]
        lift_ref[rows, span_cols] = moved[:CHUNK, :DK].astype(BF)
        fresh_state = last * state + moved[CHUNK:]
        carry[h, :, :DK] = fresh_state[:, :DK]
        carry[h, :, DK:] = fresh_state[:, DK:] + part[CHUNK:, DK:]

    @pl.when(step == pl.num_programs(0) - 1)
    def _():
        pieces = map_ref.shape[0] // value_heads
        width = DK // pieces
        for h in heads:
            moves = (carry[h, :, :DK] - ident).astype(BF)
            ends = carry[h, :, DK:].T.astype(BF)
            for p in range(pieces):
                map_ref[h * pieces + p, :DK] = moves
                map_ref[h * pieces + p, DK:] = ends[p * width:(p + 1) * width]


def run_blocks(x, weights, rate, shift, key_heads, value_heads, span, takers):
    count, depth = x.shape
    total = weights.shape[1]
    width = value_heads * DK
    map_rows = DK + DK * value_heads // takers
    whole = lambda shape: pl.BlockSpec(shape, lambda i: (0,) * len(shape))
    return pl.pallas_call(
        functools.partial(block_kernel, key_heads, value_heads, span),
        grid=(count // ROWS,),
        in_specs=[
            pl.BlockSpec((ROWS, depth), lambda i: (i, 0)),
            pl.BlockSpec((depth, total), lambda i: (0, 0), pipeline_mode=pl.Buffered(1)),
            whole((1, LANES)),
            whole((1, LANES)),
        ],
        out_specs=[
            pl.BlockSpec((ROWS, width), lambda i: (i, 0)),
            pl.BlockSpec((ROWS, width), lambda i: (i, 0)),
            whole((takers, map_rows, DK)),
        ],
        out_shape=[
            jax.ShapeDtypeStruct((count, width), F32),
            jax.ShapeDtypeStruct((count, width), BF),
            jax.ShapeDtypeStruct((takers, map_rows, DK), BF),
        ],
        scratch_shapes=[
            pltpu.VMEM((ROWS, total), F32),
            pltpu.VMEM((value_heads, DK, 2 * DK), F32),
        ],
        compiler_params=pltpu.CompilerParams(
            dimension_semantics=("arbitrary",), vmem_limit_bytes=48 * 1024 * 1024
        ),
        cost_estimate=pl.CostEstimate(
            flops=2 * count * depth * total + 2 * count * width * 2600,
            bytes_accessed=2 * count * depth + 2 * depth * total + 6 * count * width,
            transcendentals=count * value_heads * DK,
        ),
    )(x, weights, rate, shift)


def scan_kernel(maps_ref, states_ref):
    count, rows = maps_ref.shape[:2]
    held = jnp.zeros((rows - DK, DK), F32)
    for i in range(count):
        states_ref[i, 0] = held.astype(BF)
        high = held.astype(BF).astype(F32)
        both = jnp.concatenate([high, held - high], axis=0).astype(BF)
        moved = dot_nt(both, maps_ref[i, :DK])
        held = held + (moved[:rows - DK] + moved[rows - DK:]) + maps_ref[i, DK:].astype(F32)
    for i in range(count):
        states_ref[i, 1] = held.astype(BF)


def run_scan(maps):
    count, rows = maps.shape[:2]
    return pl.pallas_call(
        scan_kernel,
        out_shape=jax.ShapeDtypeStruct((count, 2, rows - DK, DK), BF),
        in_specs=[pl.BlockSpec(memory_space=pltpu.VMEM)],
        out_specs=pl.BlockSpec(memory_space=pltpu.VMEM),
        compiler_params=pltpu.CompilerParams(vmem_limit_bytes=16 * 1024 * 1024),
    )(maps)


def gather_kernel(count, own_ref, all_ref, own_sem, send_sems, recv_sems):
    size = own_ref.shape[0]
    me = lax.axis_index("seq")
    grp = lax.axis_index("grp")
    depth = count // 4
    z, place = lax.div(me, 4), lax.rem(me, 4)
    y, core = lax.div(place, 2), lax.rem(place, 2)
    across = z * 4 + (1 - y) * 2 + core
    twin = z * 4 + y * 2 + (1 - core)
    above, below = me + 4, me - 4

    def rows(block):
        return pl.ds(pl.multiple_of(block * size, size), size)

    def copy(block, way, target, source=None):
        return pltpu.make_async_remote_copy(
            src_ref=all_ref.at[rows(block)] if source is None else source,
            dst_ref=all_ref.at[rows(block)],
            send_sem=send_sems.at[block, way],
            recv_sem=recv_sems.at[block],
            device_id=(target, grp),
            device_id_type=pl.DeviceIdType.MESH,
        )

    def arrived(block):
        copy(block, 3, twin).wait_recv()

    barrier = pltpu.get_barrier_semaphore()

    def greet(target):
        pl.semaphore_signal(
            barrier, inc=1, device_id=(target, grp), device_id_type=pl.DeviceIdType.MESH
        )

    greet(across)
    greet(twin)

    @pl.when(z < depth - 1)
    def _():
        greet(above)

    @pl.when(z > 0)
    def _():
        greet(below)

    pl.semaphore_wait(
        barrier, 2 + jnp.where(z < depth - 1, 1, 0) + jnp.where(z > 0, 1, 0)
    )

    mine = pltpu.make_async_copy(own_ref, all_ref.at[rows(me)], own_sem)
    mine.start()

    @pl.when(z < depth - 1)
    def _():
        copy(me, 0, above, own_ref).start()

    @pl.when(z > 0)
    def _():
        copy(me, 1, below, own_ref).start()

    copy(me, 2, across, own_ref).start()
    copy(me, 3, twin, own_ref).start()

    for hop in range(1, depth):
        low, high = me - 4 * hop, me + 4 * hop

        @pl.when(z >= hop)
        def _():
            arrived(low)

            @pl.when(z < depth - 1)
            def _():
                copy(low, 0, above).start()

            copy(low, 2, across).start()
            copy(low, 3, twin).start()

        @pl.when(z + hop < depth)
        def _():
            arrived(high)

            @pl.when(z > 0)
            def _():
                copy(high, 1, below).start()

            copy(high, 2, across).start()
            copy(high, 3, twin).start()

        if hop == 1:
            arrived(across)
            copy(across, 3, twin).start()
        else:
            pass_on(across, hop - 1, z, depth, arrived, copy, twin)
    pass_on(across, depth - 1, z, depth, arrived, copy, twin)

    other = 1 - core
    for block in range(depth * 2):
        arrived(block * 2 + other)
    mine.wait()
    for up in range(depth):
        block = up * 4 + y * 2 + core

        @pl.when((up <= z) & (z < depth - 1))
        def _():
            copy(block, 0, above).wait_send()

        @pl.when((up >= z) & (z > 0))
        def _():
            copy(block, 1, below).wait_send()

        copy(block, 2, across).wait_send()
        copy(block, 3, twin).wait_send()
        copy(up * 4 + (1 - y) * 2 + core, 3, twin).wait_send()


def pass_on(across, hop, z, depth, arrived, copy, twin):
    @pl.when(z >= hop)
    def _():
        arrived(across - 4 * hop)
        copy(across - 4 * hop, 3, twin).start()

    @pl.when(z + hop < depth)
    def _():
        arrived(across + 4 * hop)
        copy(across + 4 * hop, 3, twin).start()


def run_gather(own, count):
    return pl.pallas_call(
        functools.partial(gather_kernel, count),
        out_shape=jax.ShapeDtypeStruct((count * own.shape[0], own.shape[1]), own.dtype),
        in_specs=[pl.BlockSpec(memory_space=pl.ANY)],
        out_specs=pl.BlockSpec(memory_space=pl.ANY),
        scratch_shapes=[
            pltpu.SemaphoreType.DMA,
            pltpu.SemaphoreType.DMA((count, 4)),
            pltpu.SemaphoreType.DMA((count,)),
        ],
        compiler_params=pltpu.CompilerParams(collective_id=0, has_side_effects=True),
        cost_estimate=pl.CostEstimate(
            flops=0, bytes_accessed=8 * count * own.size, transcendentals=0
        ),
    )(own)


def finish_kernel(out_ref, lift_ref, state_ref, gain_ref, done_ref):
    for h in range(state_ref.shape[0]):
        cols = slice(h * DK, (h + 1) * DK)
        o = out_ref[:, cols] + dot_nt(lift_ref[:, cols], state_ref[h])
        mean = jnp.mean(o * o, axis=-1, keepdims=True)
        done_ref[:, cols] = (o * lax.rsqrt(mean + 1e-06) * gain_ref[...]).astype(BF)


def run_finish(out, lifted, state, gain):
    count, width = out.shape
    rows = pl.BlockSpec((ROWS, width), lambda i: (i, 0))
    return pl.pallas_call(
        finish_kernel,
        grid=(count // ROWS,),
        in_specs=[
            rows,
            rows,
            pl.BlockSpec(state.shape, lambda i: (0, 0, 0)),
            pl.BlockSpec((1, DK), lambda i: (0, 0)),
        ],
        out_specs=rows,
        out_shape=jax.ShapeDtypeStruct((count, width), BF),
        compiler_params=pltpu.CompilerParams(
            dimension_semantics=("arbitrary",), vmem_limit_bytes=32 * 1024 * 1024
        ),
        cost_estimate=pl.CostEstimate(
            flops=2 * count * width * DK, bytes_accessed=8 * count * width, transcendentals=0
        ),
    )(out, lifted, state, gain)


def shards(
    n_seq,
    n_grp,
    prompt_tokens,
    response_tokens,
    w_query,
    w_key,
    w_value,
    w_decay,
    w_beta,
    decay_rate,
    beta_shift,
    out_gain,
    resp_lengths,
):
    value_heads = w_decay.shape[1]
    key_heads = w_key.shape[1] // DK
    grp = lax.axis_index("grp")
    pad = LANES - 2 * value_heads
    first_head = grp * value_heads
    rate = lax.dynamic_slice_in_dim(decay_rate, first_head, value_heads)
    shift = lax.dynamic_slice_in_dim(beta_shift, first_head, value_heads)
    rate = jnp.pad(rate, (0, LANES - value_heads)).reshape(1, LANES)
    shift = jnp.pad(shift, (value_heads, pad)).reshape(1, LANES)
    gain = out_gain.reshape(1, DK)
    columns = jnp.concatenate(
        [w_query, w_key, w_value, w_decay, w_beta, jnp.zeros((w_decay.shape[0], pad), BF)], axis=1
    )
    weights = run_gather(columns, n_seq)
    length, depth = response_tokens.shape[2:]
    tokens = lax.all_gather(response_tokens.reshape(length, depth), "grp", axis=0, tiled=True)

    blocks = prompt_tokens.shape[0] // ROWS
    out, lifted, own_map = run_blocks(
        prompt_tokens, weights, rate, shift, key_heads, value_heads, blocks, n_seq
    )
    maps = lax.all_to_all(own_map, "seq", split_axis=0, concat_axis=0, tiled=True)
    r_out, r_lifted, _ = run_blocks(
        tokens, weights, rate, shift, key_heads, value_heads, length // ROWS, value_heads
    )
    maps, r_out, r_lifted = lax.optimization_barrier((maps, r_out, r_lifted))
    states = lax.all_to_all(run_scan(maps), "seq", split_axis=0, concat_axis=0, tiled=True)
    start = states[:, 0].reshape(value_heads, DK, DK)
    end = states[:, 1].reshape(value_heads, DK, DK)
    r_done = run_finish(r_out, r_lifted, end, gain).reshape(n_grp, length, -1)
    prompt_output = run_finish(out, lifted, start, gain)
    exchanged = lax.all_to_all(r_done, "grp", split_axis=0, concat_axis=0, tiled=True)
    finished = jnp.swapaxes(exchanged, 0, 1).reshape(length, -1)
    positions = lax.broadcasted_iota(jnp.int32, (length, 1), 0)
    masked = jnp.where(positions < resp_lengths.reshape(()), finished, jnp.zeros_like(finished))
    return (prompt_output, masked.reshape(1, 1, length, masked.shape[1]))


def solution(mesh):
    placed = (
        P("seq", None),
        P("grp", "seq", None, None),
        P("seq", "grp"),
        P("seq", "grp"),
        P("seq", "grp"),
        P("seq", "grp"),
        P("seq", "grp"),
        P(),
        P(),
        P(),
        P("grp", "seq"),
    )
    return jax.shard_map(
        functools.partial(shards, mesh.shape["seq"], mesh.shape["grp"]),
        mesh=mesh,
        in_specs=placed,
        out_specs=(P("seq", "grp"), P("grp", "seq", None, None)),
        check_vma=False,
    )
```

```python
import functools

import jax
import jax.numpy as jnp
from jax import lax
from jax.experimental import pallas as pl
from jax.experimental.pallas import tpu as pltpu
from jax.sharding import PartitionSpec as P

DK = 128
CHUNK = 128
ROWS = 256
LANES = 128
BF = jnp.bfloat16
F32 = jnp.float32


def dot(a, b):
    return jnp.dot(a, b, preferred_element_type=F32)


def dot_nt(a, b):
    return lax.dot_general(a, b, (((1,), (1,)), ((), ())), preferred_element_type=F32)


def block_kernel(
    key_heads, value_heads, span, x_ref, w_ref, rate_ref, shift_ref,
    out_ref, lift_ref, map_ref, raw, carry,
):
    repeat = value_heads // key_heads
    step = pl.program_id(0)
    heads = range(value_heads)
    row = lax.broadcasted_iota(jnp.int32, (CHUNK, CHUNK), 0)
    col = lax.broadcasted_iota(jnp.int32, (CHUNK, CHUNK), 1)
    ident = jnp.where(row == col, 1.0, 0.0).astype(F32)

    @pl.when(lax.rem(step, span) == 0)
    def _():
        for h in heads:
            carry[h, :, :DK] = ident
            carry[h, :, DK:] = jnp.zeros((DK, DK), F32)

    x = x_ref[...]
    total = w_ref.shape[1]
    for at in range(0, total, 512):
        size = min(512, total - at)
        raw[:, at:at + size] = dot(x, w_ref[:, at:at + size])

    within = row >= col
    differ = row ^ col
    lower_ones = jnp.where(within, 1.0, 0.0).astype(F32)
    masks = []
    size = 2
    while size < CHUNK:
        masks.append(
            jnp.where((differ >= size) & (differ < 2 * size) & within, 1.0, 0.0).astype(BF)
        )
        size *= 2

    chunks = range(x_ref.shape[0] // CHUNK)
    both_of = [(c, h) for c in chunks for h in heads]
    gates_of, queries, keys, keys_t, dots = [], {}, {}, {}, {}
    for c in chunks:
        rows = slice(c * CHUNK, (c + 1) * CHUNK)
        gates = raw[rows, total - LANES:]
        log_decay = -rate_ref[...] * jax.nn.softplus(gates)
        beta = jax.nn.sigmoid(gates + shift_ref[...])
        cumul = jnp.dot(
            lower_ones, log_decay, preferred_element_type=F32, precision=lax.Precision.HIGHEST
        )
        cumul_t = cumul.T
        gates_of.append(
            (
                beta,
                beta.T,
                cumul,
                cumul_t,
                jnp.exp(cumul),
                jnp.exp(cumul_t),
                jnp.exp(cumul_t[:, CHUNK - 1:] - cumul_t),
            )
        )
        for j in range(key_heads):
            q = raw[rows, j * DK:(j + 1) * DK]
            k = raw[rows, (key_heads + j) * DK:(key_heads + j + 1) * DK]
            q = q * lax.rsqrt(jnp.sum(q * q, axis=-1, keepdims=True) + 1e-06) * DK ** (-0.5)
            k = k * lax.rsqrt(jnp.sum(k * k, axis=-1, keepdims=True) + 1e-06)
            q, k = q.astype(BF), k.astype(BF)
            queries[c, j] = q.astype(F32)
            keys[c, j] = k
            keys_t[c, j] = k.astype(F32).T
            dots[c, j] = dot_nt(jnp.concatenate([q, k], axis=0), k)

    lowers, inverses, scores = {}, {}, {}
    for c, h in both_of:
        beta, _, cumul, cumul_t = gates_of[c][:4]
        both = dots[c, h // repeat]
        spread = cumul[:, h:h + 1] - cumul_t[h:h + 1, :]
        decay = jnp.where(within, jnp.exp(spread), 0.0)
        scores[c, h] = (decay * both[:CHUNK]).astype(BF)
        lower = jnp.where(
            differ > 0,
            beta[:, value_heads + h:value_heads + h + 1] * decay * both[CHUNK:],
            0.0,
        )
        inverses[c, h] = ident - jnp.where(differ == 1, lower, 0.0)
        lowers[c, h] = lower.astype(BF)
    for mask in masks:
        small = {i: inverses[i].astype(BF) for i in both_of}
        mids = {i: dot(lowers[i] * mask, small[i]).astype(BF) for i in both_of}
        inverses = {i: inverses[i] - dot(small[i], mids[i]) for i in both_of}

    solved, parts = {}, {}
    for c, h in both_of:
        beta_t, factor_t = gates_of[c][1], gates_of[c][5]
        scaled = inverses[c, h] * beta_t[value_heads + h:value_heads + h + 1, :]
        at = (2 * key_heads + h) * DK
        values = raw[c * CHUNK:(c + 1) * CHUNK, at:at + DK].astype(BF)
        fresh = dot(scaled.astype(BF), values)
        weights = dot((scaled * factor_t[h:h + 1, :]).astype(BF), keys[c, h // repeat])
        solved[c, h] = jnp.concatenate([weights, fresh], axis=1).astype(BF)
    for c, h in both_of:
        tail_t = gates_of[c][6]
        tails = (keys_t[c, h // repeat] * tail_t[h:h + 1, :]).astype(BF)
        parts[c, h] = dot(jnp.concatenate([scores[c, h], tails], axis=0), solved[c, h])
    for c, h in both_of:
        factor = gates_of[c][4]
        rows, span_cols = slice(c * CHUNK, (c + 1) * CHUNK), slice(h * DK, (h + 1) * DK)
        part = parts[c, h]
        lifted = factor[:, h:h + 1] * queries[c, h // repeat] - part[:CHUNK, :DK]
        state = carry[h]
        left = jnp.concatenate([lifted, -part[CHUNK:, :DK]], axis=0).astype(BF)
        moved = dot(left, state.astype(BF))
        last = factor[CHUNK - 1:, h:h + 1]
        out_ref[rows, span_cols] = moved[:CHUNK, DK:] + part[:CHUNK, DK:]
        lift_ref[rows, span_cols] = moved[:CHUNK, :DK].astype(BF)
        fresh_state = last * state + moved[CHUNK:]
        carry[h, :, :DK] = fresh_state[:, :DK]
        carry[h, :, DK:] = fresh_state[:, DK:] + part[CHUNK:, DK:]

    @pl.when(step == pl.num_programs(0) - 1)
    def _():
        pieces = map_ref.shape[0] // value_heads
        width = DK // pieces
        for h in heads:
            moves = (carry[h, :, :DK] - ident).astype(BF)
            ends = carry[h, :, DK:].T.astype(BF)
            for p in range(pieces):
                map_ref[h * pieces + p, :DK] = moves
                map_ref[h * pieces + p, DK:] = ends[p * width:(p + 1) * width]


def run_blocks(x, weights, rate, shift, key_heads, value_heads, span, takers, tall):
    count, depth = x.shape
    total = weights.shape[1]
    width = value_heads * DK
    map_rows = DK + DK * value_heads // takers
    whole = lambda shape: pl.BlockSpec(shape, lambda i: (0,) * len(shape))
    return pl.pallas_call(
        functools.partial(block_kernel, key_heads, value_heads, span),
        grid=(count // tall,),
        in_specs=[
            pl.BlockSpec((tall, depth), lambda i: (i, 0)),
            pl.BlockSpec((depth, total), lambda i: (0, 0), pipeline_mode=pl.Buffered(1)),
            whole((1, LANES)),
            whole((1, LANES)),
        ],
        out_specs=[
            pl.BlockSpec((tall, width), lambda i: (i, 0)),
            pl.BlockSpec((tall, width), lambda i: (i, 0)),
            whole((takers, map_rows, DK)),
        ],
        out_shape=[
            jax.ShapeDtypeStruct((count, width), F32),
            jax.ShapeDtypeStruct((count, width), BF),
            jax.ShapeDtypeStruct((takers, map_rows, DK), BF),
        ],
        scratch_shapes=[
            pltpu.VMEM((tall, total), F32),
            pltpu.VMEM((value_heads, DK, 2 * DK), F32),
        ],
        compiler_params=pltpu.CompilerParams(
            dimension_semantics=("arbitrary",), vmem_limit_bytes=48 * 1024 * 1024
        ),
        cost_estimate=pl.CostEstimate(
            flops=2 * count * depth * total + 2 * count * width * 2600,
            bytes_accessed=2 * count * depth + 2 * depth * total + 6 * count * width,
            transcendentals=count * value_heads * DK,
        ),
    )(x, weights, rate, shift)


def scan_kernel(maps_ref, states_ref):
    count, rows = maps_ref.shape[:2]
    held = jnp.zeros((rows - DK, DK), F32)
    for i in range(count):
        states_ref[i, 0] = held.astype(BF)
        high = held.astype(BF).astype(F32)
        both = jnp.concatenate([high, held - high], axis=0).astype(BF)
        moved = dot_nt(both, maps_ref[i, :DK])
        held = held + (moved[:rows - DK] + moved[rows - DK:]) + maps_ref[i, DK:].astype(F32)
    for i in range(count):
        states_ref[i, 1] = held.astype(BF)


def run_scan(maps):
    count, rows = maps.shape[:2]
    return pl.pallas_call(
        scan_kernel,
        out_shape=jax.ShapeDtypeStruct((count, 2, rows - DK, DK), BF),
        in_specs=[pl.BlockSpec(memory_space=pltpu.VMEM)],
        out_specs=pl.BlockSpec(memory_space=pltpu.VMEM),
        compiler_params=pltpu.CompilerParams(vmem_limit_bytes=16 * 1024 * 1024),
    )(maps)


def gather_kernel(count, own_ref, all_ref, own_sem, send_sems, recv_sems):
    size = own_ref.shape[0]
    me = lax.axis_index("seq")
    grp = lax.axis_index("grp")
    depth = count // 4
    z, place = lax.div(me, 4), lax.rem(me, 4)
    y, core = lax.div(place, 2), lax.rem(place, 2)
    across = z * 4 + (1 - y) * 2 + core
    twin = z * 4 + y * 2 + (1 - core)
    above, below = me + 4, me - 4

    def rows(block):
        return pl.ds(pl.multiple_of(block * size, size), size)

    def copy(block, way, target, source=None):
        return pltpu.make_async_remote_copy(
            src_ref=all_ref.at[rows(block)] if source is None else source,
            dst_ref=all_ref.at[rows(block)],
            send_sem=send_sems.at[block, way],
            recv_sem=recv_sems.at[block],
            device_id=(target, grp),
            device_id_type=pl.DeviceIdType.MESH,
        )

    def arrived(block):
        copy(block, 3, twin).wait_recv()

    barrier = pltpu.get_barrier_semaphore()

    def greet(target):
        pl.semaphore_signal(
            barrier, inc=1, device_id=(target, grp), device_id_type=pl.DeviceIdType.MESH
        )

    greet(across)
    greet(twin)

    @pl.when(z < depth - 1)
    def _():
        greet(above)

    @pl.when(z > 0)
    def _():
        greet(below)

    pl.semaphore_wait(
        barrier, 2 + jnp.where(z < depth - 1, 1, 0) + jnp.where(z > 0, 1, 0)
    )

    mine = pltpu.make_async_copy(own_ref, all_ref.at[rows(me)], own_sem)
    mine.start()

    @pl.when(z < depth - 1)
    def _():
        copy(me, 0, above, own_ref).start()

    @pl.when(z > 0)
    def _():
        copy(me, 1, below, own_ref).start()

    copy(me, 2, across, own_ref).start()
    copy(me, 3, twin, own_ref).start()

    for hop in range(1, depth):
        low, high = me - 4 * hop, me + 4 * hop

        @pl.when(z >= hop)
        def _():
            arrived(low)

            @pl.when(z < depth - 1)
            def _():
                copy(low, 0, above).start()

            copy(low, 2, across).start()
            copy(low, 3, twin).start()

        @pl.when(z + hop < depth)
        def _():
            arrived(high)

            @pl.when(z > 0)
            def _():
                copy(high, 1, below).start()

            copy(high, 2, across).start()
            copy(high, 3, twin).start()

        if hop == 1:
            arrived(across)
            copy(across, 3, twin).start()
        else:
            pass_on(across, hop - 1, z, depth, arrived, copy, twin)
    pass_on(across, depth - 1, z, depth, arrived, copy, twin)

    other = 1 - core
    for block in range(depth * 2):
        arrived(block * 2 + other)
    mine.wait()
    for up in range(depth):
        block = up * 4 + y * 2 + core

        @pl.when((up <= z) & (z < depth - 1))
        def _():
            copy(block, 0, above).wait_send()

        @pl.when((up >= z) & (z > 0))
        def _():
            copy(block, 1, below).wait_send()

        copy(block, 2, across).wait_send()
        copy(block, 3, twin).wait_send()
        copy(up * 4 + (1 - y) * 2 + core, 3, twin).wait_send()


def pass_on(across, hop, z, depth, arrived, copy, twin):
    @pl.when(z >= hop)
    def _():
        arrived(across - 4 * hop)
        copy(across - 4 * hop, 3, twin).start()

    @pl.when(z + hop < depth)
    def _():
        arrived(across + 4 * hop)
        copy(across + 4 * hop, 3, twin).start()


def run_gather(own, count):
    return pl.pallas_call(
        functools.partial(gather_kernel, count),
        out_shape=jax.ShapeDtypeStruct((count * own.shape[0], own.shape[1]), own.dtype),
        in_specs=[pl.BlockSpec(memory_space=pl.ANY)],
        out_specs=pl.BlockSpec(memory_space=pl.ANY),
        scratch_shapes=[
            pltpu.SemaphoreType.DMA,
            pltpu.SemaphoreType.DMA((count, 4)),
            pltpu.SemaphoreType.DMA((count,)),
        ],
        compiler_params=pltpu.CompilerParams(collective_id=0, has_side_effects=True),
        cost_estimate=pl.CostEstimate(
            flops=0, bytes_accessed=8 * count * own.size, transcendentals=0
        ),
    )(own)


def finish_kernel(out_ref, lift_ref, state_ref, gain_ref, done_ref):
    for h in range(state_ref.shape[0]):
        cols = slice(h * DK, (h + 1) * DK)
        o = out_ref[:, cols] + dot_nt(lift_ref[:, cols], state_ref[h])
        mean = jnp.mean(o * o, axis=-1, keepdims=True)
        done_ref[:, cols] = (o * lax.rsqrt(mean + 1e-06) * gain_ref[...]).astype(BF)


def run_finish(out, lifted, state, gain):
    count, width = out.shape
    rows = pl.BlockSpec((ROWS, width), lambda i: (i, 0))
    return pl.pallas_call(
        finish_kernel,
        grid=(count // ROWS,),
        in_specs=[
            rows,
            rows,
            pl.BlockSpec(state.shape, lambda i: (0, 0, 0)),
            pl.BlockSpec((1, DK), lambda i: (0, 0)),
        ],
        out_specs=rows,
        out_shape=jax.ShapeDtypeStruct((count, width), BF),
        compiler_params=pltpu.CompilerParams(
            dimension_semantics=("arbitrary",), vmem_limit_bytes=32 * 1024 * 1024
        ),
        cost_estimate=pl.CostEstimate(
            flops=2 * count * width * DK, bytes_accessed=8 * count * width, transcendentals=0
        ),
    )(out, lifted, state, gain)


def shards(
    n_seq,
    n_grp,
    prompt_tokens,
    response_tokens,
    w_query,
    w_key,
    w_value,
    w_decay,
    w_beta,
    decay_rate,
    beta_shift,
    out_gain,
    resp_lengths,
):
    value_heads = w_decay.shape[1]
    key_heads = w_key.shape[1] // DK
    grp = lax.axis_index("grp")
    pad = LANES - 2 * value_heads
    first_head = grp * value_heads
    rate = lax.dynamic_slice_in_dim(decay_rate, first_head, value_heads)
    shift = lax.dynamic_slice_in_dim(beta_shift, first_head, value_heads)
    rate = jnp.pad(rate, (0, LANES - value_heads)).reshape(1, LANES)
    shift = jnp.pad(shift, (value_heads, pad)).reshape(1, LANES)
    gain = out_gain.reshape(1, DK)
    columns = jnp.concatenate(
        [w_query, w_key, w_value, w_decay, w_beta, jnp.zeros((w_decay.shape[0], pad), BF)], axis=1
    )
    weights = run_gather(columns, n_seq)
    length, depth = response_tokens.shape[2:]
    tokens = lax.all_gather(response_tokens.reshape(length, depth), "grp", axis=0, tiled=True)

    tall = 2 * ROWS if prompt_tokens.shape[0] % (2 * ROWS) == 0 else ROWS
    blocks = prompt_tokens.shape[0] // tall
    out, lifted, own_map = run_blocks(
        prompt_tokens, weights, rate, shift, key_heads, value_heads, blocks, n_seq, tall
    )
    maps = lax.all_to_all(own_map, "seq", split_axis=0, concat_axis=0, tiled=True)
    r_out, r_lifted, _ = run_blocks(
        tokens, weights, rate, shift, key_heads, value_heads, length // ROWS, value_heads, ROWS
    )
    maps, r_out, r_lifted = lax.optimization_barrier((maps, r_out, r_lifted))
    states = lax.all_to_all(run_scan(maps), "seq", split_axis=0, concat_axis=0, tiled=True)
    start = states[:, 0].reshape(value_heads, DK, DK)
    end = states[:, 1].reshape(value_heads, DK, DK)
    r_done = run_finish(r_out, r_lifted, end, gain).reshape(n_grp, length, -1)
    prompt_output = run_finish(out, lifted, start, gain)
    exchanged = lax.all_to_all(r_done, "grp", split_axis=0, concat_axis=0, tiled=True)
    finished = jnp.swapaxes(exchanged, 0, 1).reshape(length, -1)
    positions = lax.broadcasted_iota(jnp.int32, (length, 1), 0)
    masked = jnp.where(positions < resp_lengths.reshape(()), finished, jnp.zeros_like(finished))
    return (prompt_output, masked.reshape(1, 1, length, masked.shape[1]))


def solution(mesh):
    placed = (
        P("seq", None),
        P("grp", "seq", None, None),
        P("seq", "grp"),
        P("seq", "grp"),
        P("seq", "grp"),
        P("seq", "grp"),
        P("seq", "grp"),
        P(),
        P(),
        P(),
        P("grp", "seq"),
    )
    return jax.shard_map(
        functools.partial(shards, mesh.shape["seq"], mesh.shape["grp"]),
        mesh=mesh,
        in_specs=placed,
        out_specs=(P("seq", "grp"), P("grp", "seq", None, None)),
        check_vma=False,
    )
```
